32 devices in a mesh: blk: 8 (over y, x, core), col: 4 (over z).
Axes of the slice: x: 2, y: 2, z: 4, core: 2. Of those that a mesh axis runs over, the one named last changes fastest.
Arguments:
- tile_u: bfloat16 [8, 16, 1024, 128], P('blk', 'col'), may hold values from -6 to 6
- tile_v: bfloat16 [8, 16, 1024, 128], P('blk', 'col'), may hold values from -6 to 6
- tile_rank: int32 [8, 16], P('blk', 'col'), may hold values from 32 to 128
- panel_u: bfloat16 [16, 1024, 128], P('col', 'blk'), may hold values from -6 to 6
- panel_v: bfloat16 [16, 1024, 128], P('col', 'blk'), may hold values from -0.1875 to 0.1875
- band_rank: int32 [16], P('col'), may hold values from 32 to 128
- row_u: bfloat16 [8, 1024, 128], P('blk', 'col'), may hold values from -6 to 6
- row_v: bfloat16 [8, 1024, 128], P('blk', 'col'), may hold values from -0.5 to 0.5
- row_rank: int32 [8], P('blk'), may hold values from 32 to 128
- target_rank: int32 [8, 16], P('blk', 'col'), may hold values from 32 to 128
Outputs:
- new_u: bfloat16 [8, 16, 1024, 128], P('blk', 'col')
- new_v: bfloat16 [8, 16, 1024, 128], P('blk', 'col')
The draws below stay inside these ranges and needn't reach their ends.
All inputs are finite; a program needn't handle non-finite values.
Results may differ from the reference program's by a relative error of at most 0.001.
Values may be sent and summed in bfloat16 or wider, within the bound.
A program may use at most 64 MiB of HBM per device.

```python
import math
import jax
import jax.numpy as jnp
from jax import lax

NB = 1024
K = 128
BAND = 16
ROWS = 8


def with_ends(result, stream_key, smallest, largest):
    shape = result.shape
    index_at = [jax.random.randint(jax.random.fold_in(stream_key, axis), (), 0, shape[axis]) for axis in range(len(shape))]
    result = result.at[tuple(index_at)].set(smallest)
    longest = shape.index(max(shape))
    index_at[longest] = (index_at[longest] + 1) % shape[longest]
    return result.at[tuple(index_at)].set(largest)


def block_scale(rng, shape, shards, smallest, largest):
    level, own = 1.0, jax.random.fold_in(rng, 6)
    for axis_at, blocks in shards:
        steps = jnp.exp(jax.random.uniform(jax.random.fold_in(own, axis_at), (blocks,), jnp.float32, smallest / len(shards), largest / len(shards)))
        level = level * jnp.repeat(steps, shape[axis_at] // blocks).reshape([-1 if axis == axis_at else 1 for axis in range(len(shape))])
    return level


def gaussian(own_key, shape, width, limit, split=(), kind=jnp.bfloat16):
    drawn = width * jax.random.normal(own_key, shape, jnp.float32)
    if split:
        drawn = drawn * block_scale(own_key, shape, split, -0.22, 0.18)
    return jnp.clip(drawn, -limit, limit).astype(kind)


def setup_inputs(seed: int = 0) -> dict:
    streams_of = jax.random.split(jax.random.key(seed), 11)
    tile_u = gaussian(streams_of[0], (ROWS, BAND, NB, K), 1.0, 6.0, ((0, 8), (1, 4)))
    tile_v = gaussian(streams_of[1], (ROWS, BAND, NB, K), 1.0, 6.0, ((0, 8), (1, 4)))
    tile_rank = with_ends(jax.random.randint(streams_of[2], (ROWS, BAND), K // 4, K + 1), jax.random.fold_in(streams_of[2], 1), K // 4, K).astype(jnp.int32)
    panel_u = gaussian(streams_of[3], (BAND, NB, K), 1.0, 6.0, ((0, 4), (1, 8)))
    panel_v = gaussian(streams_of[4], (BAND, NB, K), NB ** -0.5, 0.1875, ((0, 4), (1, 8)))
    band_rank = with_ends(jax.random.randint(streams_of[5], (BAND,), K // 4, K + 1), jax.random.fold_in(streams_of[5], 1), K // 4, K).astype(jnp.int32)
    row_u = gaussian(streams_of[6], (ROWS, NB, K), 1.0, 6.0, ((0, 8), (1, 4)))
    row_v = gaussian(streams_of[7], (ROWS, NB, K), K ** -0.5, 0.5, ((0, 8), (1, 4)))
    row_rank = with_ends(jax.random.randint(streams_of[8], (ROWS,), K // 4, K + 1), jax.random.fold_in(streams_of[8], 1), K // 4, K).astype(jnp.int32)
    target_rank = with_ends(jax.random.randint(streams_of[9], (ROWS, BAND), K // 4, K + 1), jax.random.fold_in(streams_of[9], 1), K // 4, K).astype(jnp.int32)
    return dict(tile_u=tile_u, tile_v=tile_v, tile_rank=tile_rank, panel_u=panel_u, panel_v=panel_v, band_rank=band_rank, row_u=row_u, row_v=row_v, row_rank=row_rank, target_rank=target_rank)


HIGH = lax.Precision.HIGHEST

def pair_columns(first, second):
    joined = jnp.stack([first, second], axis=-1)
    return joined.reshape(joined.shape[:-2] + (joined.shape[-2] * 2,))

def one_row(items, panel_u, panel_v, band_rank):
    tile_u, tile_v, tile_rank, row_u, row_v, row_rank, target_rank = items
    lane = jnp.arange(K)
    row_keep = (lane < row_rank).astype(jnp.bfloat16)
    tile_keep = (lane[None, :] < tile_rank[:, None]).astype(jnp.bfloat16)
    band_keep = (lane[None, :] < band_rank[:, None]).astype(jnp.bfloat16)
    left_row = row_u * row_keep[None, :]
    right_row = (row_v * row_keep[None, :]).astype(jnp.float32)
    left_tile = tile_u * tile_keep[:, None, :]
    right_tile = (tile_v * tile_keep[:, None, :]).astype(jnp.float32)
    pu_masked = (panel_u * band_keep[:, None, :]).astype(jnp.float32)
    pv_masked = (panel_v * band_keep[:, None, :]).astype(jnp.float32)
    core = jnp.einsum('nk,jnl->jkl', right_row, pv_masked, precision=HIGH)
    right_panel = -jnp.einsum('jnl,jkl->jnk', pu_masked, core, precision=HIGH)
    left = pair_columns(left_tile, jnp.broadcast_to(left_row, left_tile.shape))
    right = pair_columns(right_tile, right_panel)
    spare = 1.0 - pair_columns(tile_keep.astype(jnp.float32), jnp.broadcast_to(row_keep.astype(jnp.float32), tile_keep.shape))
    gram = jnp.einsum('jnk,jnl->jkl', left.astype(jnp.float32), left.astype(jnp.float32), preferred_element_type=jnp.float32)
    gram = gram + spare[:, :, None] * jnp.eye(2 * K, dtype=jnp.float32)[None]
    lower = jnp.linalg.cholesky(gram)
    ortho = lax.linalg.triangular_solve(lower, left.astype(jnp.float32), left_side=False, lower=True, transpose_a=True)
    target_keep = (lane[None, :] < target_rank[:, None]).astype(jnp.float32)
    scale = math.sqrt(NB)
    new_u = ortho[:, :, :K] * scale * target_keep[:, None, :]
    head = jnp.transpose(lower, (0, 2, 1))[:, :K, :]
    new_v = jnp.einsum('jnc,jmc->jnm', right, head, precision=HIGH) / scale
    new_v = new_v * target_keep[:, None, :]
    return (new_u.astype(jnp.bfloat16), new_v.astype(jnp.bfloat16))

def reference(tile_u, tile_v, tile_rank, panel_u, panel_v, band_rank, row_u, row_v, row_rank, target_rank):

    def step(items):
        return one_row(items, panel_u, panel_v, band_rank)
    return lax.map(step, (tile_u, tile_v, tile_rank, row_u, row_v, row_rank, target_rank))
```

```python
import functools
import math

import jax
import jax.numpy as jnp
from jax import lax
from jax.experimental import pallas as pl
from jax.experimental.pallas import tpu as pltpu
from jax.sharding import PartitionSpec as P

HIGH = lax.Precision.HIGHEST
MESH = pl.DeviceIdType.MESH
F32 = jnp.float32
BF16 = jnp.bfloat16
SUB = 8
SUPER = 32


def flip(value, mask):
    bit = 1
    while bit <= mask:
        if mask & bit:
            value = value + bit - 2 * bit * ((value // bit) % 2)
        bit *= 2
    return value


def gather_kernel(
    n_blk, n_col, ru, rv, pu, pv, all_ru, all_rv, all_pu, all_pv,
    own_sem, col_send, col_recv, blk_send, blk_recv, pair_send, pair_recv,
):
    b, c = lax.axis_index("blk"), lax.axis_index("col")
    group, side = b // 2, b % 2
    groups = n_blk // 2
    sibling = group * 2 + 1 - side

    barrier = pltpu.get_barrier_semaphore()
    for step in range(1, n_col):
        pl.semaphore_signal(barrier, inc=1, device_id=(b, (c + step) % n_col), device_id_type=MESH)
    for step in range(1, groups):
        pl.semaphore_signal(
            barrier, inc=1, device_id=(flip(group, step) * 2 + side, c), device_id_type=MESH
        )
    pl.semaphore_signal(barrier, inc=1, device_id=(sibling, c), device_id_type=MESH)
    pl.semaphore_wait(barrier, n_col - 1 + groups - 1 + 1)

    rows = ((ru, all_ru), (rv, all_rv))
    panels = ((pv, all_pv), (pu, all_pu))
    row_copies, blk_copies, pair_copies, own_copies = [], [], [], []
    for at, (source, whole) in enumerate(rows):
        for step in range(1, n_col):
            copy = pltpu.make_async_remote_copy(
                src_ref=source.at[0],
                dst_ref=whole.at[c],
                send_sem=col_send.at[at, step],
                recv_sem=col_recv.at[at, step],
                device_id=(b, (c + step) % n_col),
                device_id_type=MESH,
            )
            copy.start()
            row_copies.append(copy)
    for at, (source, whole) in enumerate(panels):
        for step in range(1, groups):
            copy = pltpu.make_async_remote_copy(
                src_ref=source,
                dst_ref=whole.at[b],
                send_sem=blk_send.at[at, step],
                recv_sem=blk_recv.at[at, step],
                device_id=(flip(group, step) * 2 + side, c),
                device_id_type=MESH,
            )
            copy.start()
            blk_copies.append((at, step, whole, copy))
        copy = pltpu.make_async_remote_copy(
            src_ref=source,
            dst_ref=whole.at[b],
            send_sem=pair_send.at[at, 0],
            recv_sem=pair_recv.at[at, 0],
            device_id=(sibling, c),
            device_id_type=MESH,
        )
        copy.start()
        pair_copies.append(copy)
    for at, (source, target) in enumerate(
        ((ru.at[0], all_ru.at[c]), (rv.at[0], all_rv.at[c]), (pv, all_pv.at[b]), (pu, all_pu.at[b]))
    ):
        copy = pltpu.make_async_copy(source, target, own_sem.at[at])
        copy.start()
        own_copies.append(copy)
    for at, step, whole, copy in blk_copies:
        copy.wait_recv()
        origin = flip(group, step) * 2 + side
        onward = pltpu.make_async_remote_copy(
            src_ref=whole.at[origin],
            dst_ref=whole.at[origin],
            send_sem=pair_send.at[at, step],
            recv_sem=pair_recv.at[at, step],
            device_id=(sibling, c),
            device_id_type=MESH,
        )
        onward.start()
        pair_copies.append(onward)
    for copy in own_copies:
        copy.wait()
    for copy in row_copies:
        copy.wait()
    for _, _, _, copy in blk_copies:
        copy.wait_send()
    for copy in pair_copies:
        copy.wait()


def gather(n_blk, n_col, row_u, row_v, panel_u, panel_v):
    groups = n_blk // 2
    any_space = pl.BlockSpec(memory_space=pl.ANY)
    row_shape = (n_col,) + row_u.shape[1:]
    panel_shape = (n_blk,) + panel_u.shape
    dma = pltpu.SemaphoreType.DMA
    return pl.pallas_call(
        functools.partial(gather_kernel, n_blk, n_col),
        out_shape=[jax.ShapeDtypeStruct(row_shape, BF16)] * 2
        + [jax.ShapeDtypeStruct(panel_shape, BF16)] * 2,
        in_specs=[any_space] * 4,
        out_specs=[any_space] * 4,
        scratch_shapes=[
            dma((4,)),
            dma((2, n_col)),
            dma((2, n_col)),
            dma((2, groups)),
            dma((2, groups)),
            dma((2, groups)),
            dma((2, groups)),
        ],
        compiler_params=pltpu.CompilerParams(collective_id=0, has_side_effects=True),
        name="gather",
    )(row_u, row_v, panel_u, panel_v)


def across(first, second, precision=None):
    return lax.dot_general(
        first, second, (((0,), (0,)), ((), ())), precision=precision, preferred_element_type=F32
    )


def split(value):
    high = value.astype(BF16)
    return high, (value - high.astype(F32)).astype(BF16)


def eliminate(work, width, tiles):
    lane = lax.broadcasted_iota(jnp.int32, (SUB, width), 1)

    def spread(row, at):
        return jnp.broadcast_to(row[:, at : at + 1], (SUB, width))

    for top in range(0, width, SUPER):
        for base in range(top, top + SUPER, SUB):
            within = (lane >= base) & (lane < base + SUB)
            rows = [work[pl.ds((base + i) * SUB, SUB), :] for i in range(SUB)]
            entry = {
                (i, j): spread(rows[i], base + j) for i in range(SUB) for j in range(i, SUB)
            }
            rows = [
                jnp.where(within, (lane == base + i).astype(F32), rows[i]) for i in range(SUB)
            ]
            for k in range(SUB):
                inverse = lax.rsqrt(entry[k, k])
                rows[k] = rows[k] * inverse
                factor = {j: entry[k, j] * inverse for j in range(k + 1, SUB)}
                for i in range(k + 1, SUB):
                    for j in range(i, SUB):
                        entry[i, j] = entry[i, j] - factor[i] * factor[j]
                for i in range(k + 1, SUB):
                    rows[i] = rows[i] - factor[i] * rows[k]
            for i in range(SUB):
                work[pl.ds((base + i) * SUB, SUB), :] = rows[i]
            for i in range(base + SUB, top + SUPER):
                row = jnp.where(within, 0.0, work[pl.ds(i * SUB, SUB), :])
                for k in range(SUB):
                    row = row - spread(rows[k], i) * rows[k]
                work[pl.ds(i * SUB, SUB), :] = row
        below = top + SUPER
        if below < width:
            rest = width - below
            column = lax.broadcasted_iota(jnp.int32, (rest, width), 1)
            done = (column >= top) & (column < below)
            pivot = lax.broadcasted_iota(jnp.int32, (SUPER, width), 0) + top
            ahead = lax.broadcasted_iota(jnp.int32, (SUPER, width), 1)
            ahead = (ahead > pivot) & (ahead < below)
            for t in range(tiles):
                pivots = work[pl.ds(top * SUB + t, SUPER, stride=SUB), :]
                update = across(pivots, jnp.where(ahead, 0.0, pivots), HIGH)[below:, :]
                old = work[pl.ds(below * SUB + t, rest, stride=SUB), :]
                work[pl.ds(below * SUB + t, rest, stride=SUB), :] = (
                    jnp.where(done, 0.0, old) - update
                )


def tile_kernel(
    tile_rank, band_rank, row_rank, target_rank,
    tile_u, tile_v, all_ru, all_rv, all_pu, all_pv, new_u, new_v,
    work, left, gram_t, gram_r,
):
    tiles, order, width = tile_u.shape[1:]
    half = width // 2
    scale = math.sqrt(order)
    row = lax.broadcasted_iota(jnp.int32, (width, width), 0)
    col = lax.broadcasted_iota(jnp.int32, (width, width), 1)
    place = col // 2
    even = col % 2 == 0
    ru = all_ru[...]
    rv = all_rv[...]
    rr = row_rank[0]
    for t in range(tiles):
        tr = tile_rank[0, t]
        tu = tile_u[0, t]
        pick_t = ((row == place) & even & (row < tr)).astype(BF16)
        pick_r = ((row == place) & jnp.logical_not(even) & (row < rr)).astype(BF16)
        both = jnp.concatenate([tu, ru], axis=1)
        first = jnp.dot(
            both, jnp.concatenate([pick_t, pick_r], axis=0), preferred_element_type=F32
        ).astype(BF16)
        left[t] = first
        gram_t[t] = across(tu, first)
        gram_r[t] = across(ru, first)
        spare = (row == col) & (place >= jnp.where(even, tr, rr))
        work[pl.ds(t, width, stride=SUB), :] = across(first, first) + spare.astype(F32)
    eliminate(work, width, tiles)
    for t in range(tiles):
        keep = col < target_rank[0, t]
        inverse = jnp.where(col <= row, work[pl.ds(t, width, stride=SUB), :], 0.0).T
        inverse = jnp.where(keep, inverse, 0.0)
        high, low = split(inverse * scale)
        first = left[t]
        new_u[0, t] = jnp.dot(
            jnp.concatenate([first, first], axis=1),
            jnp.concatenate([high, low], axis=0),
            preferred_element_type=F32,
        ).astype(BF16)
        pv = all_pv[:, t].reshape(order, width)
        pu = all_pu[:, t].reshape(order, width)
        core = jnp.where(row < rr, across(rv, pv), 0.0)
        head_t = jnp.dot(gram_t[t], inverse, precision=HIGH, preferred_element_type=F32)
        head_r = jnp.dot(gram_r[t], inverse, precision=HIGH, preferred_element_type=F32)
        panel = across(core, head_r, HIGH)
        head_t = jnp.where(row < tile_rank[0, t], head_t, 0.0) / scale
        panel = jnp.where(row < band_rank[t], -panel, 0.0) / scale
        high, low = split(jnp.concatenate([head_t, panel], axis=0))
        right = jnp.concatenate([tile_v[0, t], pu], axis=1)
        new_v[0, t] = (
            jnp.dot(right, high, preferred_element_type=F32)
            + jnp.dot(right, low, preferred_element_type=F32)
        ).astype(BF16)


def update(tile_u, tile_v, tile_rank, all_pu, all_pv, band_rank, all_ru, all_rv, row_rank, target_rank):
    tiles, order, width = tile_u.shape[1:]
    smem = pl.BlockSpec(memory_space=pltpu.SMEM)
    vmem = pl.BlockSpec(memory_space=pltpu.VMEM)
    return pl.pallas_call(
        tile_kernel,
        out_shape=[jax.ShapeDtypeStruct(tile_u.shape, BF16)] * 2,
        in_specs=[smem] * 4 + [vmem] * 6,
        out_specs=[vmem] * 2,
        scratch_shapes=[
            pltpu.VMEM((width * SUB, width), F32),
            pltpu.VMEM((tiles, order, width), BF16),
            pltpu.VMEM((tiles, width, width), F32),
            pltpu.VMEM((tiles, width, width), F32),
        ],
        compiler_params=pltpu.CompilerParams(vmem_limit_bytes=48 * 1024 * 1024),
        name="tiles",
    )(tile_rank, band_rank, row_rank, target_rank, tile_u, tile_v, all_ru, all_rv, all_pu, all_pv)


def on_device(
    n_blk, n_col,
    tile_u, tile_v, tile_rank, panel_u, panel_v, band_rank, row_u, row_v, row_rank, target_rank,
):
    order, width = tile_u.shape[2:]
    all_ru, all_rv, all_pu, all_pv = gather(n_blk, n_col, row_u, row_v, panel_u, panel_v)
    all_ru, all_rv = all_ru.reshape(order, width), all_rv.reshape(order, width)
    if panel_u.shape[1] % 16:
        all_pu, all_pv = (
            jnp.swapaxes(each, 0, 1).reshape(1, each.shape[1], order, width)
            for each in (all_pu, all_pv)
        )
    return tuple(
        update(
            tile_u, tile_v, tile_rank, all_pu, all_pv, band_rank, all_ru, all_rv, row_rank,
            target_rank,
        )
    )


def solution(mesh):
    return jax.shard_map(
        functools.partial(on_device, mesh.shape["blk"], mesh.shape["col"]),
        mesh=mesh,
        in_specs=(
            P("blk", "col", None, None),
            P("blk", "col", None, None),
            P("blk", "col"),
            P("col", "blk", None),
            P("col", "blk", None),
            P("col"),
            P("blk", "col", None),
            P("blk", "col", None),
            P("blk"),
            P("blk", "col"),
        ),
        out_specs=(P("blk", "col", None, None), P("blk", "col", None, None)),
        check_vma=False,
    )
```

```python
import functools
import math

import jax
import jax.numpy as jnp
from jax import lax
from jax.experimental import pallas as pl
from jax.experimental.pallas import tpu as pltpu
from jax.sharding import PartitionSpec as P

HIGH = lax.Precision.HIGHEST
MESH = pl.DeviceIdType.MESH
F32 = jnp.float32
BF16 = jnp.bfloat16
SUB = 8
SUPER = 32


def flip(value, mask):
    bit = 1
    while bit <= mask:
        if mask & bit:
            value = value + bit - 2 * bit * ((value // bit) % 2)
        bit *= 2
    return value


def gather_kernel(
    n_blk, n_col, ru, rv, pu, pv, all_ru, all_rv, all_pu, all_pv,
    own_sem, col_send, col_recv, blk_send, blk_recv, pair_send, pair_recv,
):
    b, c = lax.axis_index("blk"), lax.axis_index("col")
    group, side = b // 2, b % 2
    groups = n_blk // 2
    sibling = group * 2 + 1 - side

    barrier = pltpu.get_barrier_semaphore()
    for step in range(1, n_col):
        pl.semaphore_signal(barrier, inc=1, device_id=(b, (c + step) % n_col), device_id_type=MESH)
    for step in range(1, groups):
        pl.semaphore_signal(
            barrier, inc=1, device_id=(flip(group, step) * 2 + side, c), device_id_type=MESH
        )
    pl.semaphore_signal(barrier, inc=1, device_id=(sibling, c), device_id_type=MESH)
    pl.semaphore_wait(barrier, n_col - 1 + groups - 1 + 1)

    rows = ((ru, all_ru), (rv, all_rv))
    panels = ((pv, all_pv), (pu, all_pu))
    row_copies, blk_copies, pair_copies, own_copies = [], [], [], []
    for at, (source, whole) in enumerate(rows):
        for step in range(1, n_col):
            copy = pltpu.make_async_remote_copy(
                src_ref=source.at[0],
                dst_ref=whole.at[c],
                send_sem=col_send.at[at, step],
                recv_sem=col_recv.at[at, step],
                device_id=(b, (c + step) % n_col),
                device_id_type=MESH,
            )
            copy.start()
            row_copies.append(copy)
    for at, (source, whole) in enumerate(panels):
        for step in range(1, groups):
            copy = pltpu.make_async_remote_copy(
                src_ref=source,
                dst_ref=whole.at[b],
                send_sem=blk_send.at[at, step],
                recv_sem=blk_recv.at[at, step],
                device_id=(flip(group, step) * 2 + side, c),
                device_id_type=MESH,
            )
            copy.start()
            blk_copies.append((at, step, whole, copy))
        copy = pltpu.make_async_remote_copy(
            src_ref=source,
            dst_ref=whole.at[b],
            send_sem=pair_send.at[at, 0],
            recv_sem=pair_recv.at[at, 0],
            device_id=(sibling, c),
            device_id_type=MESH,
        )
        copy.start()
        pair_copies.append(copy)
    for at, (source, target) in enumerate(
        ((ru.at[0], all_ru.at[c]), (rv.at[0], all_rv.at[c]), (pv, all_pv.at[b]), (pu, all_pu.at[b]))
    ):
        copy = pltpu.make_async_copy(source, target, own_sem.at[at])
        copy.start()
        own_copies.append(copy)
    for at, step, whole, copy in blk_copies:
        copy.wait_recv()
        origin = flip(group, step) * 2 + side
        onward = pltpu.make_async_remote_copy(
            src_ref=whole.at[origin],
            dst_ref=whole.at[origin],
            send_sem=pair_send.at[at, step],
            recv_sem=pair_recv.at[at, step],
            device_id=(sibling, c),
            device_id_type=MESH,
        )
        onward.start()
        pair_copies.append(onward)
    for copy in own_copies:
        copy.wait()
    for copy in row_copies:
        copy.wait()
    for _, _, _, copy in blk_copies:
        copy.wait_send()
    for copy in pair_copies:
        copy.wait()


def gather(n_blk, n_col, row_u, row_v, panel_u, panel_v):
    groups = n_blk // 2
    any_space = pl.BlockSpec(memory_space=pl.ANY)
    row_shape = (n_col,) + row_u.shape[1:]
    panel_shape = (n_blk,) + panel_u.shape
    dma = pltpu.SemaphoreType.DMA
    return pl.pallas_call(
        functools.partial(gather_kernel, n_blk, n_col),
        out_shape=[jax.ShapeDtypeStruct(row_shape, BF16)] * 2
        + [jax.ShapeDtypeStruct(panel_shape, BF16)] * 2,
        in_specs=[any_space] * 4,
        out_specs=[any_space] * 4,
        scratch_shapes=[
            dma((4,)),
            dma((2, n_col)),
            dma((2, n_col)),
            dma((2, groups)),
            dma((2, groups)),
            dma((2, groups)),
            dma((2, groups)),
        ],
        compiler_params=pltpu.CompilerParams(collective_id=0, has_side_effects=True),
        name="gather",
    )(row_u, row_v, panel_u, panel_v)


def across(first, second, precision=None):
    return lax.dot_general(
        first, second, (((0,), (0,)), ((), ())), precision=precision, preferred_element_type=F32
    )


def first_half(t, tu, ru, tr, rr, left, gram_t, gram_r, work):
    width = tu.shape[1]
    row = lax.broadcasted_iota(jnp.int32, (width, width), 0)
    col = lax.broadcasted_iota(jnp.int32, (width, width), 1)
    place = col // 2
    even = col % 2 == 0
    pick_t = ((row == place) & even & (row < tr)).astype(BF16)
    pick_r = ((row == place) & jnp.logical_not(even) & (row < rr)).astype(BF16)
    both = jnp.concatenate([tu, ru], axis=1)
    first = jnp.dot(
        both, jnp.concatenate([pick_t, pick_r], axis=0), preferred_element_type=F32
    ).astype(BF16)
    left[t] = first
    gram_t[t] = across(tu, first)
    gram_r[t] = across(ru, first)
    spare = (row == col) & (place >= jnp.where(even, tr, rr))
    work[pl.ds(t, width, stride=SUB), :] = across(first, first) + spare.astype(F32)


def factors(t, scale, ranks, core, gram_t, gram_r, work):
    tr, br, tk = ranks
    width = core.shape[0]
    row = lax.broadcasted_iota(jnp.int32, (width, width), 0)
    col = lax.broadcasted_iota(jnp.int32, (width, width), 1)
    inverse = jnp.where(col <= row, work[pl.ds(t, width, stride=SUB), :], 0.0).T
    inverse = jnp.where(col < tk, inverse, 0.0)
    head_t = jnp.dot(gram_t[t], inverse, precision=HIGH, preferred_element_type=F32)
    head_r = jnp.dot(gram_r[t], inverse, precision=HIGH, preferred_element_type=F32)
    panel = across(core, head_r, HIGH)
    head_t = jnp.where(row < tr, head_t, 0.0) / scale
    panel = jnp.where(row < br, -panel, 0.0) / scale
    return split(inverse * scale), split(jnp.concatenate([head_t, panel], axis=0))


def split(value):
    high = value.astype(BF16)
    return high, (value - high.astype(F32)).astype(BF16)


def eliminate(work, width, tiles, between={}):
    lane = lax.broadcasted_iota(jnp.int32, (SUB, width), 1)

    def spread(row, at):
        return jnp.broadcast_to(row[:, at : at + 1], (SUB, width))

    for top in range(0, width, SUPER):
        if top in between:
            between[top]()
        for base in range(top, top + SUPER, SUB):
            within = (lane >= base) & (lane < base + SUB)
            rows = [work[pl.ds((base + i) * SUB, SUB), :] for i in range(SUB)]
            entry = {
                (i, j): spread(rows[i], base + j) for i in range(SUB) for j in range(i, SUB)
            }
            rows = [
                jnp.where(within, (lane == base + i).astype(F32), rows[i]) for i in range(SUB)
            ]
            for k in range(SUB):
                inverse = lax.rsqrt(entry[k, k])
                rows[k] = rows[k] * inverse
                factor = {j: entry[k, j] * inverse for j in range(k + 1, SUB)}
                for i in range(k + 1, SUB):
                    for j in range(i, SUB):
                        entry[i, j] = entry[i, j] - factor[i] * factor[j]
                for i in range(k + 1, SUB):
                    rows[i] = rows[i] - factor[i] * rows[k]
            for i in range(SUB):
                work[pl.ds((base + i) * SUB, SUB), :] = rows[i]
            for i in range(base + SUB, top + SUPER):
                row = jnp.where(within, 0.0, work[pl.ds(i * SUB, SUB), :])
                for k in range(SUB):
                    row = row - spread(rows[k], i) * rows[k]
                work[pl.ds(i * SUB, SUB), :] = row
        below = top + SUPER
        if below < width:
            rest = width - below
            column = lax.broadcasted_iota(jnp.int32, (rest, width), 1)
            done = (column >= top) & (column < below)
            pivot = lax.broadcasted_iota(jnp.int32, (SUPER, width), 0) + top
            ahead = lax.broadcasted_iota(jnp.int32, (SUPER, width), 1)
            ahead = (ahead > pivot) & (ahead < below)
            for t in range(tiles):
                pivots = work[pl.ds(top * SUB + t, SUPER, stride=SUB), :]
                update = across(pivots, jnp.where(ahead, 0.0, pivots), HIGH)[below:, :]
                old = work[pl.ds(below * SUB + t, rest, stride=SUB), :]
                work[pl.ds(below * SUB + t, rest, stride=SUB), :] = (
                    jnp.where(done, 0.0, old) - update
                )


def products(first, u_parts, tv, pu, v_parts):
    new_u = jnp.dot(
        jnp.concatenate([first, first], axis=1), u_parts, preferred_element_type=F32
    ).astype(BF16)
    right = jnp.concatenate([tv, pu], axis=1)
    new_v = (
        jnp.dot(right, v_parts[0], preferred_element_type=F32)
        + jnp.dot(right, v_parts[1], preferred_element_type=F32)
    ).astype(BF16)
    return new_u, new_v


def tile_kernel(
    tile_rank, band_rank, row_rank, target_rank,
    tile_u, tile_v, all_ru, all_rv, all_pu, all_pv, new_u, new_v,
    work, left, gram_t, gram_r,
):
    tiles, order, width = tile_u.shape[1:]
    ru = all_ru[...]
    rv = all_rv[...]
    rr = row_rank[0]
    row = lax.broadcasted_iota(jnp.int32, (width, width), 0)
    for t in range(tiles):
        first_half(t, tile_u[0, t], ru, tile_rank[0, t], rr, left, gram_t, gram_r, work)
    eliminate(work, width, tiles)
    for t in range(tiles):
        core = jnp.where(row < rr, across(rv, all_pv[:, t].reshape(order, width)), 0.0)
        ranks = (tile_rank[0, t], band_rank[t], target_rank[0, t])
        u_parts, v_parts = factors(t, math.sqrt(order), ranks, core, gram_t, gram_r, work)
        new_u[0, t], new_v[0, t] = products(
            left[t], jnp.concatenate(u_parts, axis=0), tile_v[0, t],
            all_pu[:, t].reshape(order, width), v_parts,
        )


def factor_kernel(
    n_blk, n_col, tile_rank, band_rank, row_rank, target_rank, tile_u, ru, rv, pu, pv,
    all_pu, left_out, u_out, v_out,
    tu, all_ru, all_rv, all_pv, left, work, gram_t, gram_r, cores,
    own_sem, tile_sem, left_sem, col_send, col_recv, blk_send, blk_recv, pair_send, pair_recv,
):
    tiles, order, width = tu.shape
    b, c = lax.axis_index("blk"), lax.axis_index("col")
    group, side = b // 2, b % 2
    sibling = group * 2 + 1 - side
    near = {step: flip(group, step) * 2 + side for step in (1, 2, 3)}

    locals_ = [
        pltpu.make_async_copy(ru.at[0], all_ru.at[c], own_sem.at[0]),
        pltpu.make_async_copy(rv.at[0], all_rv.at[c], own_sem.at[1]),
        pltpu.make_async_copy(pv, all_pv.at[b], own_sem.at[2]),
        pltpu.make_async_copy(pu, all_pu.at[b], own_sem.at[3]),
    ]
    tile_copies = [
        pltpu.make_async_copy(tile_u.at[0, t], tu.at[t], tile_sem.at[t]) for t in range(tiles)
    ]
    for copy in locals_ + tile_copies:
        copy.start()

    barrier = pltpu.get_barrier_semaphore()
    peers = [(b, (c + step) % n_col) for step in range(1, n_col)]
    peers += [(near[1], c), (near[2], c), (sibling, c)]
    for peer in peers:
        pl.semaphore_signal(barrier, inc=1, device_id=peer, device_id_type=MESH)
    pl.semaphore_wait(barrier, len(peers))

    def row_sends(at, source, whole):
        copies = [
            pltpu.make_async_remote_copy(
                src_ref=source.at[0],
                dst_ref=whole.at[c],
                send_sem=col_send.at[at, step],
                recv_sem=col_recv.at[at, step],
                device_id=(b, (c + step) % n_col),
                device_id_type=MESH,
            )
            for step in range(1, n_col)
        ]
        for copy in copies:
            copy.start()
        return copies

    def panel_send(at, step, source, whole, slot, target, send, recv):
        copy = pltpu.make_async_remote_copy(
            src_ref=source,
            dst_ref=whole.at[slot],
            send_sem=send.at[at, step],
            recv_sem=recv.at[at, step],
            device_id=(target, c),
            device_id_type=MESH,
        )
        copy.start()
        return copy

    ru_copies = row_sends(0, ru, all_ru)
    wholes = (all_pv, all_pu)
    blk_copies, pair_copies = {}, []
    for at, source in enumerate((pv, pu)):
        for step in (1, 2):
            blk_copies[at, step] = panel_send(
                at, step, source, wholes[at], b, near[step], blk_send, blk_recv
            )
    for at, source in enumerate((pv, pu)):
        pair_copies.append(
            panel_send(at, 0, source, wholes[at], b, sibling, pair_send, pair_recv)
        )

    def pass_on(at, step):
        blk_copies[at, step].wait_recv()
        slot = near[step]
        here = wholes[at].at[slot]
        if (at, step) == (0, 2):
            blk_copies[0, 3] = panel_send(0, 3, here, all_pv, slot, near[1], blk_send, blk_recv)
        if (at, step) == (1, 1):
            blk_copies[1, 3] = panel_send(1, 3, here, all_pu, slot, near[2], blk_send, blk_recv)
        pair_copies.append(
            panel_send(at, step, here, wholes[at], slot, sibling, pair_send, pair_recv)
        )

    locals_[0].wait()
    for copy in ru_copies:
        copy.wait_recv()
    rv_copies = row_sends(1, rv, all_rv)
    ru_all = all_ru[...].reshape(order, width)
    rr = row_rank[0]
    left_copies = []
    for t in range(tiles):
        tile_copies[t].wait()
        first_half(t, tu[t], ru_all, tile_rank[0, t], rr, left, gram_t, gram_r, work)
        if t == tiles // 2 - 1:
            for at, step in ((0, 2), (1, 1), (0, 1), (1, 2)):
                pass_on(at, step)
    for t in range(tiles):
        copy = pltpu.make_async_copy(left.at[t], left_out.at[t], left_sem.at[t])
        copy.start()
        left_copies.append(copy)

    def diagonal():
        pass_on(0, 3)
        pass_on(1, 3)

    def cores_ready():
        row = lax.broadcasted_iota(jnp.int32, (width, width), 0)
        for copy in locals_[1:]:
            copy.wait()
        for copy in rv_copies + pair_copies:
            copy.wait_recv()
        rv_all = all_rv[...].reshape(order, width)
        for t in range(tiles):
            cores[t] = jnp.where(
                row < rr, across(rv_all, all_pv[:, t].reshape(order, width)), 0.0
            )

    eliminate(work, width, tiles, {SUPER: diagonal, 3 * SUPER: cores_ready})
    for t in range(tiles):
        ranks = (tile_rank[0, t], band_rank[t], target_rank[0, t])
        u_parts, v_parts = factors(t, math.sqrt(order), ranks, cores[t], gram_t, gram_r, work)
        u_out[t] = jnp.concatenate(u_parts, axis=0)
        v_out[t, 0], v_out[t, 1] = v_parts
    for copy in left_copies:
        copy.wait()
    for copy in ru_copies + rv_copies + list(blk_copies.values()) + pair_copies:
        copy.wait_send()


def factor(n_blk, n_col, tile_u, tile_rank, panel_u, panel_v, band_rank, row_u, row_v, row_rank, target_rank):
    tiles, order, width = tile_u.shape[1:]
    smem = pl.BlockSpec(memory_space=pltpu.SMEM)
    vmem = pl.BlockSpec(memory_space=pltpu.VMEM)
    any_space = pl.BlockSpec(memory_space=pl.ANY)
    dma = pltpu.SemaphoreType.DMA
    row_shape = (n_col,) + row_u.shape[1:]
    panel_shape = (n_blk,) + panel_u.shape
    return pl.pallas_call(
        functools.partial(factor_kernel, n_blk, n_col),
        out_shape=[
            jax.ShapeDtypeStruct(panel_shape, BF16),
            jax.ShapeDtypeStruct((tiles, order, width), BF16),
            jax.ShapeDtypeStruct((tiles, 2 * width, width), BF16),
            jax.ShapeDtypeStruct((tiles, 2, 2 * width, width), BF16),
        ],
        in_specs=[smem] * 4 + [any_space] * 5,
        out_specs=[any_space] * 2 + [vmem] * 2,
        scratch_shapes=[
            pltpu.VMEM((tiles, order, width), BF16),
            pltpu.VMEM(row_shape, BF16),
            pltpu.VMEM(row_shape, BF16),
            pltpu.VMEM(panel_shape, BF16),
            pltpu.VMEM((tiles, order, width), BF16),
            pltpu.VMEM((width * SUB, width), F32),
            pltpu.VMEM((tiles, width, width), F32),
            pltpu.VMEM((tiles, width, width), F32),
            pltpu.VMEM((tiles, width, width), F32),
            dma((4,)),
            dma((tiles,)),
            dma((tiles,)),
            dma((2, n_col)),
            dma((2, n_col)),
            dma((2, 4)),
            dma((2, 4)),
            dma((2, 4)),
            dma((2, 4)),
        ],
        compiler_params=pltpu.CompilerParams(
            collective_id=0, has_side_effects=True, vmem_limit_bytes=32 * 1024 * 1024
        ),
        name="factor",
    )(tile_rank, band_rank, row_rank, target_rank, tile_u, row_u, row_v, panel_u, panel_v)


def product_kernel(left, u_parts, tile_v, all_pu, v_parts, new_u, new_v):
    order, width = left.shape[1:]
    new_u[0, 0], new_v[0, 0] = products(
        left[0], u_parts[0], tile_v[0, 0], all_pu[:, 0].reshape(order, width), v_parts[0]
    )


def product(left, u_parts, tile_v, all_pu, v_parts):
    tiles, order, width = left.shape
    tile = pl.BlockSpec((1, 1, order, width), lambda t: (0, t, 0, 0))
    n_blk, _, rows, _ = all_pu.shape
    return pl.pallas_call(
        product_kernel,
        grid=(tiles,),
        out_shape=[jax.ShapeDtypeStruct(tile_v.shape, BF16)] * 2,
        in_specs=[
            pl.BlockSpec((1, order, width), lambda t: (t, 0, 0)),
            pl.BlockSpec((1, 2 * width, width), lambda t: (t, 0, 0)),
            tile,
            pl.BlockSpec((n_blk, 1, rows, width), lambda t: (0, t, 0, 0)),
            pl.BlockSpec((1, 2, 2 * width, width), lambda t: (t, 0, 0, 0)),
        ],
        out_specs=[tile] * 2,
        compiler_params=pltpu.CompilerParams(vmem_limit_bytes=32 * 1024 * 1024),
        name="product",
    )(left, u_parts, tile_v, all_pu, v_parts)


def update(tile_u, tile_v, tile_rank, all_pu, all_pv, band_rank, all_ru, all_rv, row_rank, target_rank):
    tiles, order, width = tile_u.shape[1:]
    smem = pl.BlockSpec(memory_space=pltpu.SMEM)
    vmem = pl.BlockSpec(memory_space=pltpu.VMEM)
    return pl.pallas_call(
        tile_kernel,
        out_shape=[jax.ShapeDtypeStruct(tile_u.shape, BF16)] * 2,
        in_specs=[smem] * 4 + [vmem] * 6,
        out_specs=[vmem] * 2,
        scratch_shapes=[
            pltpu.VMEM((width * SUB, width), F32),
            pltpu.VMEM((tiles, order, width), BF16),
            pltpu.VMEM((tiles, width, width), F32),
            pltpu.VMEM((tiles, width, width), F32),
        ],
        compiler_params=pltpu.CompilerParams(vmem_limit_bytes=48 * 1024 * 1024),
        name="tiles",
    )(tile_rank, band_rank, row_rank, target_rank, tile_u, tile_v, all_ru, all_rv, all_pu, all_pv)


def on_device(
    n_blk, n_col,
    tile_u, tile_v, tile_rank, panel_u, panel_v, band_rank, row_u, row_v, row_rank, target_rank,
):
    order, width = tile_u.shape[2:]
    if n_blk == 8 and panel_u.shape[1] % 16 == 0:
        all_pu, left, u_parts, v_parts = factor(
            n_blk, n_col, tile_u, tile_rank, panel_u, panel_v, band_rank, row_u, row_v, row_rank,
            target_rank,
        )
        return tuple(product(left, u_parts, tile_v, all_pu, v_parts))
    all_ru, all_rv, all_pu, all_pv = gather(n_blk, n_col, row_u, row_v, panel_u, panel_v)
    all_ru, all_rv = all_ru.reshape(order, width), all_rv.reshape(order, width)
    if panel_u.shape[1] % 16:
        all_pu, all_pv = (
            jnp.swapaxes(each, 0, 1).reshape(1, each.shape[1], order, width)
            for each in (all_pu, all_pv)
        )
    return tuple(
        update(
            tile_u, tile_v, tile_rank, all_pu, all_pv, band_rank, all_ru, all_rv, row_rank,
            target_rank,
        )
    )


def solution(mesh):
    return jax.shard_map(
        functools.partial(on_device, mesh.shape["blk"], mesh.shape["col"]),
        mesh=mesh,
        in_specs=(
            P("blk", "col", None, None),
            P("blk", "col", None, None),
            P("blk", "col"),
            P("col", "blk", None),
            P("col", "blk", None),
            P("col"),
            P("blk", "col", None),
            P("blk", "col", None),
            P("blk"),
            P("blk", "col"),
        ),
        out_specs=(P("blk", "col", None, None), P("blk", "col", None, None)),
        check_vma=False,
    )
```

```python
import functools
import math

import jax
import jax.numpy as jnp
from jax import lax
from jax.experimental import pallas as pl
from jax.experimental.pallas import tpu as pltpu
from jax.sharding import PartitionSpec as P

HIGH = lax.Precision.HIGHEST
MESH = pl.DeviceIdType.MESH
F32 = jnp.float32
BF16 = jnp.bfloat16
SUB = 8
SUPER = 32


def flip(value, mask):
    bit = 1
    while bit <= mask:
        if mask & bit:
            value = value + bit - 2 * bit * ((value // bit) % 2)
        bit *= 2
    return value


def gather_kernel(
    n_blk, n_col, ru, rv, pu, pv, all_ru, all_rv, all_pu, all_pv,
    own_sem, col_send, col_recv, blk_send, blk_recv, pair_send, pair_recv,
):
    b, c = lax.axis_index("blk"), lax.axis_index("col")
    group, side = b // 2, b % 2
    groups = n_blk // 2
    sibling = group * 2 + 1 - side

    barrier = pltpu.get_barrier_semaphore()
    for step in range(1, n_col):
        pl.semaphore_signal(barrier, inc=1, device_id=(b, (c + step) % n_col), device_id_type=MESH)
    for step in range(1, groups):
        pl.semaphore_signal(
            barrier, inc=1, device_id=(flip(group, step) * 2 + side, c), device_id_type=MESH
        )
    pl.semaphore_signal(barrier, inc=1, device_id=(sibling, c), device_id_type=MESH)
    pl.semaphore_wait(barrier, n_col - 1 + groups - 1 + 1)

    rows = ((ru, all_ru), (rv, all_rv))
    panels = ((pv, all_pv), (pu, all_pu))
    row_copies, blk_copies, pair_copies, own_copies = [], [], [], []
    for at, (source, whole) in enumerate(rows):
        for step in range(1, n_col):
            copy = pltpu.make_async_remote_copy(
                src_ref=source.at[0],
                dst_ref=whole.at[c],
                send_sem=col_send.at[at, step],
                recv_sem=col_recv.at[at, step],
                device_id=(b, (c + step) % n_col),
                device_id_type=MESH,
            )
            copy.start()
            row_copies.append(copy)
    for at, (source, whole) in enumerate(panels):
        for step in range(1, groups):
            copy = pltpu.make_async_remote_copy(
                src_ref=source,
                dst_ref=whole.at[b],
                send_sem=blk_send.at[at, step],
                recv_sem=blk_recv.at[at, step],
                device_id=(flip(group, step) * 2 + side, c),
                device_id_type=MESH,
            )
            copy.start()
            blk_copies.append((at, step, whole, copy))
        copy = pltpu.make_async_remote_copy(
            src_ref=source,
            dst_ref=whole.at[b],
            send_sem=pair_send.at[at, 0],
            recv_sem=pair_recv.at[at, 0],
            device_id=(sibling, c),
            device_id_type=MESH,
        )
        copy.start()
        pair_copies.append(copy)
    for at, (source, target) in enumerate(
        ((ru.at[0], all_ru.at[c]), (rv.at[0], all_rv.at[c]), (pv, all_pv.at[b]), (pu, all_pu.at[b]))
    ):
        copy = pltpu.make_async_copy(source, target, own_sem.at[at])
        copy.start()
        own_copies.append(copy)
    for at, step, whole, copy in blk_copies:
        copy.wait_recv()
        origin = flip(group, step) * 2 + side
        onward = pltpu.make_async_remote_copy(
            src_ref=whole.at[origin],
            dst_ref=whole.at[origin],
            send_sem=pair_send.at[at, step],
            recv_sem=pair_recv.at[at, step],
            device_id=(sibling, c),
            device_id_type=MESH,
        )
        onward.start()
        pair_copies.append(onward)
    for copy in own_copies:
        copy.wait()
    for copy in row_copies:
        copy.wait()
    for _, _, _, copy in blk_copies:
        copy.wait_send()
    for copy in pair_copies:
        copy.wait()


def gather(n_blk, n_col, row_u, row_v, panel_u, panel_v):
    groups = n_blk // 2
    any_space = pl.BlockSpec(memory_space=pl.ANY)
    row_shape = (n_col,) + row_u.shape[1:]
    panel_shape = (n_blk,) + panel_u.shape
    dma = pltpu.SemaphoreType.DMA
    return pl.pallas_call(
        functools.partial(gather_kernel, n_blk, n_col),
        out_shape=[jax.ShapeDtypeStruct(row_shape, BF16)] * 2
        + [jax.ShapeDtypeStruct(panel_shape, BF16)] * 2,
        in_specs=[any_space] * 4,
        out_specs=[any_space] * 4,
        scratch_shapes=[
            dma((4,)),
            dma((2, n_col)),
            dma((2, n_col)),
            dma((2, groups)),
            dma((2, groups)),
            dma((2, groups)),
            dma((2, groups)),
        ],
        compiler_params=pltpu.CompilerParams(collective_id=0, has_side_effects=True),
        name="gather",
    )(row_u, row_v, panel_u, panel_v)


def across(first, second, precision=None):
    return lax.dot_general(
        first, second, (((0,), (0,)), ((), ())), precision=precision, preferred_element_type=F32
    )


def first_half(t, tu, ru, tr, rr, left, gram_t, gram_r, work):
    width = tu.shape[1]
    row = lax.broadcasted_iota(jnp.int32, (width, width), 0)
    col = lax.broadcasted_iota(jnp.int32, (width, width), 1)
    place = col // 2
    even = col % 2 == 0
    pick_t = ((row == place) & even & (row < tr)).astype(BF16)
    pick_r = ((row == place) & jnp.logical_not(even) & (row < rr)).astype(BF16)
    both = jnp.concatenate([tu, ru], axis=1)
    first = jnp.dot(
        both, jnp.concatenate([pick_t, pick_r], axis=0), preferred_element_type=F32
    ).astype(BF16)
    left[t] = first
    gram_t[t] = across(tu, first)
    gram_r[t] = across(ru, first)
    spare = (row == col) & (place >= jnp.where(even, tr, rr))
    work[pl.ds(t, width, stride=SUB), :] = across(first, first) + spare.astype(F32)


def factors(t, scale, ranks, core, gram_t, gram_r, work):
    tr, br, tk = ranks
    width = core.shape[0]
    row = lax.broadcasted_iota(jnp.int32, (width, width), 0)
    col = lax.broadcasted_iota(jnp.int32, (width, width), 1)
    inverse = jnp.where(col <= row, work[pl.ds(t, width, stride=SUB), :], 0.0).T
    inverse = jnp.where(col < tk, inverse, 0.0)
    head_t = jnp.dot(gram_t[t], inverse, precision=HIGH, preferred_element_type=F32)
    head_r = jnp.dot(gram_r[t], inverse, precision=HIGH, preferred_element_type=F32)
    panel = across(core, head_r, HIGH)
    head_t = jnp.where(row < tr, head_t, 0.0) / scale
    panel = jnp.where(row < br, -panel, 0.0) / scale
    return split(inverse * scale), split(jnp.concatenate([head_t, panel], axis=0))


def split(value):
    high = value.astype(BF16)
    return high, (value - high.astype(F32)).astype(BF16)


def eliminate(work, width, tiles, between={}):
    lane = lax.broadcasted_iota(jnp.int32, (SUB, width), 1)

    def spread(row, at):
        return jnp.broadcast_to(row[:, at : at + 1], (SUB, width))

    for top in range(0, width, SUPER):
        if top in between:
            between[top]()
        for base in range(top, top + SUPER, SUB):
            within = (lane >= base) & (lane < base + SUB)
            rows = [work[pl.ds((base + i) * SUB, SUB), :] for i in range(SUB)]
            entry = {
                (i, j): spread(rows[i], base + j) for i in range(SUB) for j in range(i, SUB)
            }
            rows = [
                jnp.where(within, (lane == base + i).astype(F32), rows[i]) for i in range(SUB)
            ]
            for k in range(SUB):
                inverse = lax.rsqrt(entry[k, k])
                rows[k] = rows[k] * inverse
                factor = {j: entry[k, j] * inverse for j in range(k + 1, SUB)}
                for i in range(k + 1, SUB):
                    for j in range(i, SUB):
                        entry[i, j] = entry[i, j] - factor[i] * factor[j]
                for i in range(k + 1, SUB):
                    rows[i] = rows[i] - factor[i] * rows[k]
            for i in range(SUB):
                work[pl.ds((base + i) * SUB, SUB), :] = rows[i]
            for i in range(base + SUB, top + SUPER):
                row = jnp.where(within, 0.0, work[pl.ds(i * SUB, SUB), :])
                for k in range(SUB):
                    row = row - spread(rows[k], i) * rows[k]
                work[pl.ds(i * SUB, SUB), :] = row
        below = top + SUPER
        if below < width:
            rest = width - below
            column = lax.broadcasted_iota(jnp.int32, (rest, width), 1)
            done = (column >= top) & (column < below)
            pivot = lax.broadcasted_iota(jnp.int32, (SUPER, width), 0) + top
            ahead = lax.broadcasted_iota(jnp.int32, (SUPER, width), 1)
            ahead = (ahead > pivot) & (ahead < below)
            for t in range(tiles):
                pivots = work[pl.ds(top * SUB + t, SUPER, stride=SUB), :]
                update = across(pivots, jnp.where(ahead, 0.0, pivots), HIGH)[below:, :]
                old = work[pl.ds(below * SUB + t, rest, stride=SUB), :]
                work[pl.ds(below * SUB + t, rest, stride=SUB), :] = (
                    jnp.where(done, 0.0, old) - update
                )


def products(first, u_parts, tv, pu, v_parts):
    new_u = jnp.dot(
        jnp.concatenate([first, first], axis=1), u_parts, preferred_element_type=F32
    ).astype(BF16)
    right = jnp.concatenate([tv, pu], axis=1)
    new_v = (
        jnp.dot(right, v_parts[0], preferred_element_type=F32)
        + jnp.dot(right, v_parts[1], preferred_element_type=F32)
    ).astype(BF16)
    return new_u, new_v


def tile_kernel(
    tile_rank, band_rank, row_rank, target_rank,
    tile_u, tile_v, all_ru, all_rv, all_pu, all_pv, new_u, new_v,
    work, left, gram_t, gram_r,
):
    tiles, order, width = tile_u.shape[1:]
    ru = all_ru[...]
    rv = all_rv[...]
    rr = row_rank[0]
    row = lax.broadcasted_iota(jnp.int32, (width, width), 0)
    for t in range(tiles):
        first_half(t, tile_u[0, t], ru, tile_rank[0, t], rr, left, gram_t, gram_r, work)
    eliminate(work, width, tiles)
    for t in range(tiles):
        core = jnp.where(row < rr, across(rv, all_pv[:, t].reshape(order, width)), 0.0)
        ranks = (tile_rank[0, t], band_rank[t], target_rank[0, t])
        u_parts, v_parts = factors(t, math.sqrt(order), ranks, core, gram_t, gram_r, work)
        new_u[0, t], new_v[0, t] = products(
            left[t], jnp.concatenate(u_parts, axis=0), tile_v[0, t],
            all_pu[:, t].reshape(order, width), v_parts,
        )


def factor_kernel(
    n_blk, n_col, tile_rank, band_rank, row_rank, target_rank, tile_u, ru, rv, pu, pv,
    all_pu, left_out, u_out, v_out,
    tu, own_ru, near_ru, far_ru, all_ru, all_rv, all_pv, left, work, gram_t, gram_r, cores,
    own_sem, tile_sem, left_sem, col_send, col_recv, blk_send, blk_recv, pair_send, pair_recv,
):
    tiles, order, width = tu.shape
    b, c = lax.axis_index("blk"), lax.axis_index("col")
    group, side = b // 2, b % 2
    sibling = group * 2 + 1 - side
    near = {step: flip(group, step) * 2 + side for step in (1, 2, 3)}

    locals_ = [
        pltpu.make_async_copy(ru.at[0], own_ru, own_sem.at[0]),
        pltpu.make_async_copy(rv.at[0], all_rv.at[c], own_sem.at[1]),
        pltpu.make_async_copy(pv, all_pv.at[b], own_sem.at[2]),
        pltpu.make_async_copy(pu, all_pu.at[b], own_sem.at[3]),
    ]
    tile_copies = [
        pltpu.make_async_copy(tile_u.at[0, t], tu.at[t], tile_sem.at[t]) for t in range(tiles)
    ]
    for copy in locals_ + tile_copies:
        copy.start()

    chunk = order // n_col
    part, half = chunk // 2, width // 2
    row = lax.broadcasted_iota(jnp.int32, (width, width), 0)
    col = lax.broadcasted_iota(jnp.int32, (width, width), 1)
    place = col // 2
    even = col % 2 == 0

    def one_hot(*blocks):
        return jnp.concatenate([block.astype(BF16) for block in blocks], axis=0)

    locals_[0].wait()
    mine = jnp.concatenate([own_ru[:part, :], own_ru[part:, :]], axis=1)
    low = col < half
    for whole, shift in ((near_ru, 0), (far_ru, half)):
        whole[c] = jnp.dot(
            mine,
            one_hot((row == col + shift) & low, (row == col - half + shift) & jnp.logical_not(low)),
            preferred_element_type=F32,
        ).astype(BF16)

    barrier = pltpu.get_barrier_semaphore()
    peers = [(b, (c + step) % n_col) for step in range(1, n_col)]
    peers += [(near[1], c), (near[2], c), (sibling, c)]
    for peer in peers:
        pl.semaphore_signal(barrier, inc=1, device_id=peer, device_id_type=MESH)
    pl.semaphore_wait(barrier, len(peers))

    def row_sends(at, source, whole):
        copies = [
            pltpu.make_async_remote_copy(
                src_ref=source,
                dst_ref=whole.at[c],
                send_sem=col_send.at[at, step],
                recv_sem=col_recv.at[at, step],
                device_id=(b, (c + step) % n_col),
                device_id_type=MESH,
            )
            for step in range(1, n_col)
        ]
        for copy in copies:
            copy.start()
        return copies

    def panel_send(at, step, source, whole, slot, target, send, recv):
        copy = pltpu.make_async_remote_copy(
            src_ref=source,
            dst_ref=whole.at[slot],
            send_sem=send.at[at, step],
            recv_sem=recv.at[at, step],
            device_id=(target, c),
            device_id_type=MESH,
        )
        copy.start()
        return copy

    near_copies = row_sends(0, near_ru.at[c], near_ru)
    wholes = (all_pv, all_pu)
    blk_copies, pair_copies = {}, []
    for at, source in enumerate((pv, pu)):
        for step in (1, 2):
            blk_copies[at, step] = panel_send(
                at, step, source, wholes[at], b, near[step], blk_send, blk_recv
            )
    for at, source in enumerate((pv, pu)):
        pair_copies.append(
            panel_send(at, 0, source, wholes[at], b, sibling, pair_send, pair_recv)
        )

    def pass_on(at, step):
        blk_copies[at, step].wait_recv()
        slot = near[step]
        here = wholes[at].at[slot]
        if (at, step) == (0, 2):
            blk_copies[0, 3] = panel_send(0, 3, here, all_pv, slot, near[1], blk_send, blk_recv)
        if (at, step) == (1, 1):
            blk_copies[1, 3] = panel_send(1, 3, here, all_pu, slot, near[2], blk_send, blk_recv)
        pair_copies.append(
            panel_send(at, step, here, wholes[at], slot, sibling, pair_send, pair_recv)
        )

    for copy in near_copies:
        copy.wait_recv()
    far_copies = row_sends(1, far_ru.at[c], far_ru)
    rv_copies = row_sends(2, rv.at[0], all_rv)
    rr = row_rank[0]
    left_copies = []
    for t in range(tiles):
        tr = tile_rank[0, t]
        tile_copies[t].wait()
        pick_t = (row == place) & even & (row < tr)
        for side_by in range(2):
            pick_r = (row - side_by * half == place) & jnp.logical_not(even) & (place < rr)
            starts = [q * chunk + side_by * part for q in range(n_col)]
            both = jnp.concatenate(
                [
                    jnp.concatenate([tu[t, start : start + part, :], near_ru[q]], axis=1)
                    for q, start in enumerate(starts)
                ],
                axis=0,
            )
            first = jnp.dot(both, one_hot(pick_t, pick_r), preferred_element_type=F32)
            first = first.astype(BF16)
            for q, start in enumerate(starts):
                left[t, start : start + part, :] = first[q * part : (q + 1) * part]
        first = left[t]
        spare = (row == col) & (place >= jnp.where(even, tr, rr))
        work[pl.ds(t, width, stride=SUB), :] = across(first, first) + spare.astype(F32)
    for t in range(tiles):
        copy = pltpu.make_async_copy(left.at[t], left_out.at[t], left_sem.at[t])
        copy.start()
        left_copies.append(copy)

    def neighbours():
        for at, step in ((0, 2), (1, 1), (0, 1), (1, 2)):
            pass_on(at, step)
        for t in range(tiles):
            gram_t[t] = across(tu[t], left[t])

    def row_grams():
        for copy in far_copies:
            copy.wait_recv()
        for side_by in range(2):
            back = one_hot(
                (row - side_by * half == col) & low,
                (row - side_by * half == col - half) & jnp.logical_not(low),
            )
            for q in range(n_col):
                both = jnp.concatenate([near_ru[q], far_ru[q]], axis=1)
                start = q * chunk + side_by * part
                all_ru[start : start + part, :] = jnp.dot(
                    both, back, preferred_element_type=F32
                ).astype(BF16)
        for t in range(tiles):
            gram_r[t] = across(all_ru[...], left[t])

    def diagonal():
        pass_on(0, 3)
        pass_on(1, 3)

    eliminate(
        work, width, tiles, {SUPER: neighbours, 2 * SUPER: row_grams, 3 * SUPER: diagonal}
    )
    for copy in locals_[1:]:
        copy.wait()
    for copy in rv_copies + pair_copies:
        copy.wait_recv()
    rv_all = all_rv[...].reshape(order, width)
    for t in range(tiles):
        cores[t] = jnp.where(
            row < rr, across(rv_all, all_pv[:, t].reshape(order, width)), 0.0
        )
    for t in range(tiles):
        ranks = (tile_rank[0, t], band_rank[t], target_rank[0, t])
        u_parts, v_parts = factors(t, math.sqrt(order), ranks, cores[t], gram_t, gram_r, work)
        u_out[t] = jnp.concatenate(u_parts, axis=0)
        v_out[t, 0], v_out[t, 1] = v_parts
    for copy in left_copies:
        copy.wait()
    for copy in near_copies + far_copies + rv_copies + list(blk_copies.values()) + pair_copies:
        copy.wait_send()


def factor(n_blk, n_col, tile_u, tile_rank, panel_u, panel_v, band_rank, row_u, row_v, row_rank, target_rank):
    tiles, order, width = tile_u.shape[1:]
    smem = pl.BlockSpec(memory_space=pltpu.SMEM)
    vmem = pl.BlockSpec(memory_space=pltpu.VMEM)
    any_space = pl.BlockSpec(memory_space=pl.ANY)
    dma = pltpu.SemaphoreType.DMA
    row_shape = (n_col,) + row_u.shape[1:]
    panel_shape = (n_blk,) + panel_u.shape
    packed = (n_col, row_u.shape[1] // 2, width)
    return pl.pallas_call(
        functools.partial(factor_kernel, n_blk, n_col),
        out_shape=[
            jax.ShapeDtypeStruct(panel_shape, BF16),
            jax.ShapeDtypeStruct((tiles, order, width), BF16),
            jax.ShapeDtypeStruct((tiles, 2 * width, width), BF16),
            jax.ShapeDtypeStruct((tiles, 2, 2 * width, width), BF16),
        ],
        in_specs=[smem] * 4 + [pl.BlockSpec(memory_space=pltpu.HBM)] * 5,
        out_specs=[any_space] * 2 + [vmem] * 2,
        scratch_shapes=[
            pltpu.VMEM((tiles, order, width), BF16),
            pltpu.VMEM(row_u.shape[1:], BF16),
            pltpu.VMEM(packed, BF16),
            pltpu.VMEM(packed, BF16),
            pltpu.VMEM((order, width), BF16),
            pltpu.VMEM(row_shape, BF16),
            pltpu.VMEM(panel_shape, BF16),
            pltpu.VMEM((tiles, order, width), BF16),
            pltpu.VMEM((width * SUB, width), F32),
            pltpu.VMEM((tiles, width, width), F32),
            pltpu.VMEM((tiles, width, width), F32),
            pltpu.VMEM((tiles, width, width), F32),
            dma((4,)),
            dma((tiles,)),
            dma((tiles,)),
            dma((3, n_col)),
            dma((3, n_col)),
            dma((2, 4)),
            dma((2, 4)),
            dma((2, 4)),
            dma((2, 4)),
        ],
        compiler_params=pltpu.CompilerParams(
            collective_id=0, has_side_effects=True, vmem_limit_bytes=60 * 1024 * 1024
        ),
        name="factor",
    )(tile_rank, band_rank, row_rank, target_rank, tile_u, row_u, row_v, panel_u, panel_v)


def product_kernel(left, u_parts, tile_v, all_pu, v_parts, new_u, new_v):
    order, width = left.shape[1:]
    new_u[0, 0], new_v[0, 0] = products(
        left[0], u_parts[0], tile_v[0, 0], all_pu[:, 0].reshape(order, width), v_parts[0]
    )


def product(left, u_parts, tile_v, all_pu, v_parts):
    tiles, order, width = left.shape
    tile = pl.BlockSpec((1, 1, order, width), lambda t: (0, t, 0, 0))
    n_blk, _, rows, _ = all_pu.shape
    return pl.pallas_call(
        product_kernel,
        grid=(tiles,),
        out_shape=[jax.ShapeDtypeStruct(tile_v.shape, BF16)] * 2,
        in_specs=[
            pl.BlockSpec((1, order, width), lambda t: (t, 0, 0)),
            pl.BlockSpec((1, 2 * width, width), lambda t: (t, 0, 0)),
            tile,
            pl.BlockSpec((n_blk, 1, rows, width), lambda t: (0, t, 0, 0)),
            pl.BlockSpec((1, 2, 2 * width, width), lambda t: (t, 0, 0, 0)),
        ],
        out_specs=[tile] * 2,
        compiler_params=pltpu.CompilerParams(vmem_limit_bytes=60 * 1024 * 1024),
        name="product",
    )(left, u_parts, tile_v, all_pu, v_parts)


def update(tile_u, tile_v, tile_rank, all_pu, all_pv, band_rank, all_ru, all_rv, row_rank, target_rank):
    tiles, order, width = tile_u.shape[1:]
    smem = pl.BlockSpec(memory_space=pltpu.SMEM)
    vmem = pl.BlockSpec(memory_space=pltpu.VMEM)
    return pl.pallas_call(
        tile_kernel,
        out_shape=[jax.ShapeDtypeStruct(tile_u.shape, BF16)] * 2,
        in_specs=[smem] * 4 + [vmem] * 6,
        out_specs=[vmem] * 2,
        scratch_shapes=[
            pltpu.VMEM((width * SUB, width), F32),
            pltpu.VMEM((tiles, order, width), BF16),
            pltpu.VMEM((tiles, width, width), F32),
            pltpu.VMEM((tiles, width, width), F32),
        ],
        compiler_params=pltpu.CompilerParams(vmem_limit_bytes=48 * 1024 * 1024),
        name="tiles",
    )(tile_rank, band_rank, row_rank, target_rank, tile_u, tile_v, all_ru, all_rv, all_pu, all_pv)


def on_device(
    n_blk, n_col,
    tile_u, tile_v, tile_rank, panel_u, panel_v, band_rank, row_u, row_v, row_rank, target_rank,
):
    order, width = tile_u.shape[2:]
    if n_blk == 8 and panel_u.shape[1] % 16 == 0:
        all_pu, left, u_parts, v_parts = factor(
            n_blk, n_col, tile_u, tile_rank, panel_u, panel_v, band_rank, row_u, row_v, row_rank,
            target_rank,
        )
        return tuple(product(left, u_parts, tile_v, all_pu, v_parts))
    all_ru, all_rv, all_pu, all_pv = gather(n_blk, n_col, row_u, row_v, panel_u, panel_v)
    all_ru, all_rv = all_ru.reshape(order, width), all_rv.reshape(order, width)
    if panel_u.shape[1] % 16:
        all_pu, all_pv = (
            jnp.swapaxes(each, 0, 1).reshape(1, each.shape[1], order, width)
            for each in (all_pu, all_pv)
        )
    return tuple(
        update(
            tile_u, tile_v, tile_rank, all_pu, all_pv, band_rank, all_ru, all_rv, row_rank,
            target_rank,
        )
    )


def solution(mesh):
    return jax.shard_map(
        functools.partial(on_device, mesh.shape["blk"], mesh.shape["col"]),
        mesh=mesh,
        in_specs=(
            P("blk", "col", None, None),
            P("blk", "col", None, None),
            P("blk", "col"),
            P("col", "blk", None),
            P("col", "blk", None),
            P("col"),
            P("blk", "col", None),
            P("blk", "col", None),
            P("blk"),
            P("blk", "col"),
        ),
        out_specs=(P("blk", "col", None, None), P("blk", "col", None, None)),
        check_vma=False,
    )
```

```python
import functools
import math

import jax
import jax.numpy as jnp
from jax import lax
from jax.experimental import pallas as pl
from jax.experimental.pallas import tpu as pltpu
from jax.sharding import PartitionSpec as P

MESH = pl.DeviceIdType.MESH
F32 = jnp.float32
BF16 = jnp.bfloat16
SUB = 8
SUPER = 32


def flip(value, mask):
    bit = 1
    while bit <= mask:
        if mask & bit:
            value = value + bit - 2 * bit * ((value // bit) % 2)
        bit *= 2
    return value


def gather_kernel(
    n_blk, n_col, ru, rv, pu, pv, all_ru, all_rv, all_pu, all_pv,
    own_sem, col_send, col_recv, blk_send, blk_recv, pair_send, pair_recv,
):
    b, c = lax.axis_index("blk"), lax.axis_index("col")
    group, side = b // 2, b % 2
    groups = n_blk // 2
    sibling = group * 2 + 1 - side

    barrier = pltpu.get_barrier_semaphore()
    for step in range(1, n_col):
        pl.semaphore_signal(barrier, inc=1, device_id=(b, (c + step) % n_col), device_id_type=MESH)
    for step in range(1, groups):
        pl.semaphore_signal(
            barrier, inc=1, device_id=(flip(group, step) * 2 + side, c), device_id_type=MESH
        )
    pl.semaphore_signal(barrier, inc=1, device_id=(sibling, c), device_id_type=MESH)
    pl.semaphore_wait(barrier, n_col - 1 + groups - 1 + 1)

    rows = ((ru, all_ru), (rv, all_rv))
    panels = ((pv, all_pv), (pu, all_pu))
    row_copies, blk_copies, pair_copies, own_copies = [], [], [], []
    for at, (source, whole) in enumerate(rows):
        for step in range(1, n_col):
            copy = pltpu.make_async_remote_copy(
                src_ref=source.at[0],
                dst_ref=whole.at[c],
                send_sem=col_send.at[at, step],
                recv_sem=col_recv.at[at, step],
                device_id=(b, (c + step) % n_col),
                device_id_type=MESH,
            )
            copy.start()
            row_copies.append(copy)
    for at, (source, whole) in enumerate(panels):
        for step in range(1, groups):
            copy = pltpu.make_async_remote_copy(
                src_ref=source,
                dst_ref=whole.at[b],
                send_sem=blk_send.at[at, step],
                recv_sem=blk_recv.at[at, step],
                device_id=(flip(group, step) * 2 + side, c),
                device_id_type=MESH,
            )
            copy.start()
            blk_copies.append((at, step, whole, copy))
        copy = pltpu.make_async_remote_copy(
            src_ref=source,
            dst_ref=whole.at[b],
            send_sem=pair_send.at[at, 0],
            recv_sem=pair_recv.at[at, 0],
            device_id=(sibling, c),
            device_id_type=MESH,
        )
        copy.start()
        pair_copies.append(copy)
    for at, (source, target) in enumerate(
        ((ru.at[0], all_ru.at[c]), (rv.at[0], all_rv.at[c]), (pv, all_pv.at[b]), (pu, all_pu.at[b]))
    ):
        copy = pltpu.make_async_copy(source, target, own_sem.at[at])
        copy.start()
        own_copies.append(copy)
    for at, step, whole, copy in blk_copies:
        copy.wait_recv()
        origin = flip(group, step) * 2 + side
        onward = pltpu.make_async_remote_copy(
            src_ref=whole.at[origin],
            dst_ref=whole.at[origin],
            send_sem=pair_send.at[at, step],
            recv_sem=pair_recv.at[at, step],
            device_id=(sibling, c),
            device_id_type=MESH,
        )
        onward.start()
        pair_copies.append(onward)
    for copy in own_copies:
        copy.wait()
    for copy in row_copies:
        copy.wait()
    for _, _, _, copy in blk_copies:
        copy.wait_send()
    for copy in pair_copies:
        copy.wait()


def gather(n_blk, n_col, row_u, row_v, panel_u, panel_v):
    groups = n_blk // 2
    any_space = pl.BlockSpec(memory_space=pl.ANY)
    row_shape = (n_col,) + row_u.shape[1:]
    panel_shape = (n_blk,) + panel_u.shape
    dma = pltpu.SemaphoreType.DMA
    return pl.pallas_call(
        functools.partial(gather_kernel, n_blk, n_col),
        out_shape=[jax.ShapeDtypeStruct(row_shape, BF16)] * 2
        + [jax.ShapeDtypeStruct(panel_shape, BF16)] * 2,
        in_specs=[any_space] * 4,
        out_specs=[any_space] * 4,
        scratch_shapes=[
            dma((4,)),
            dma((2, n_col)),
            dma((2, n_col)),
            dma((2, groups)),
            dma((2, groups)),
            dma((2, groups)),
            dma((2, groups)),
        ],
        compiler_params=pltpu.CompilerParams(collective_id=0, has_side_effects=True),
        name="gather",
    )(row_u, row_v, panel_u, panel_v)


def across(first, second):
    return lax.dot_general(
        first, second, (((0,), (0,)), ((), ())), preferred_element_type=F32
    )


def first_half(t, tu, ru, tr, rr, left, gram_t, gram_r, work):
    width = tu.shape[1]
    row = lax.broadcasted_iota(jnp.int32, (width, width), 0)
    col = lax.broadcasted_iota(jnp.int32, (width, width), 1)
    place = col // 2
    even = col % 2 == 0
    pick_t = ((row == place) & even & (row < tr)).astype(BF16)
    pick_r = ((row == place) & jnp.logical_not(even) & (row < rr)).astype(BF16)
    both = jnp.concatenate([tu, ru], axis=1)
    first = jnp.dot(
        both, jnp.concatenate([pick_t, pick_r], axis=0), preferred_element_type=F32
    ).astype(BF16)
    left[t] = first
    gram_t[t] = across(tu, first)
    gram_r[t] = across(ru, first)
    spare = (row == col) & (place >= jnp.where(even, tr, rr))
    work[pl.ds(t, width, stride=SUB), :] = across(first, first) + spare.astype(F32)


def factors(t, scale, ranks, core, gram_t, gram_r, work):
    tr, br, tk = ranks
    width = core.shape[0]
    row = lax.broadcasted_iota(jnp.int32, (width, width), 0)
    col = lax.broadcasted_iota(jnp.int32, (width, width), 1)
    inverse = jnp.where(col <= row, work[pl.ds(t, width, stride=SUB), :], 0.0).T
    inverse = jnp.where(col < tk, inverse, 0.0)
    grams = jnp.concatenate([gram_t[t], gram_r[t]], axis=0)
    heads = jnp.dot(*stacked(grams, inverse, 1, 0), preferred_element_type=F32)
    head_t, head_r = heads[:width], heads[width:]
    panel = across(*stacked(core, head_r, 0, 0))
    head_t = jnp.where(row < tr, head_t, 0.0) / scale
    panel = jnp.where(row < br, -panel, 0.0) / scale
    return split(inverse * scale), split(jnp.concatenate([head_t, panel], axis=0))


def split(value):
    high = value.astype(BF16)
    return high, (value - high.astype(F32)).astype(BF16)


def stacked(first, second, first_axis, second_axis):
    parts = []
    for value in (first, second):
        a = value.astype(BF16)
        rest = value - a.astype(F32)
        b = rest.astype(BF16)
        parts.append((a, b, (rest - b.astype(F32)).astype(BF16)))
    (a, b, c), (d, e, f) = parts
    return (
        jnp.concatenate([a, a, b, b, a, c], axis=first_axis),
        jnp.concatenate([d, e, d, e, f, d], axis=second_axis),
    )


def eliminate(work, width, tiles, between={}):
    lane = lax.broadcasted_iota(jnp.int32, (SUB, width), 1)

    def spread(row, at):
        return jnp.broadcast_to(row[:, at : at + 1], (SUB, width))

    for top in range(0, width, SUPER):
        if top in between:
            between[top]()
        for base in range(top, top + SUPER, SUB):
            within = (lane >= base) & (lane < base + SUB)
            rows = [work[pl.ds((base + i) * SUB, SUB), :] for i in range(SUB)]
            entry = {
                (i, j): spread(rows[i], base + j) for i in range(SUB) for j in range(i, SUB)
            }
            rows = [
                jnp.where(within, (lane == base + i).astype(F32), rows[i]) for i in range(SUB)
            ]
            for k in range(SUB):
                inverse = lax.rsqrt(entry[k, k])
                rows[k] = rows[k] * inverse
                factor = {j: entry[k, j] * inverse for j in range(k + 1, SUB)}
                for i in range(k + 1, SUB):
                    for j in range(i, SUB):
                        entry[i, j] = entry[i, j] - factor[i] * factor[j]
                for i in range(k + 1, SUB):
                    rows[i] = rows[i] - factor[i] * rows[k]
            for i in range(SUB):
                work[pl.ds((base + i) * SUB, SUB), :] = rows[i]
            for i in range(base + SUB, top + SUPER):
                row = jnp.where(within, 0.0, work[pl.ds(i * SUB, SUB), :])
                for k in range(SUB):
                    row = row - spread(rows[k], i) * rows[k]
                work[pl.ds(i * SUB, SUB), :] = row
        below = top + SUPER
        if below < width:
            rest = width - below
            column = lax.broadcasted_iota(jnp.int32, (rest, width), 1)
            done = (column >= top) & (column < below)
            pivot = lax.broadcasted_iota(jnp.int32, (SUPER, width), 0) + top
            ahead = lax.broadcasted_iota(jnp.int32, (SUPER, width), 1)
            ahead = (ahead > pivot) & (ahead < below)
            for t in range(tiles):
                pivots = work[pl.ds(top * SUB + t, SUPER, stride=SUB), :]
                update = across(*stacked(pivots, jnp.where(ahead, 0.0, pivots), 0, 0))[below:, :]
                old = work[pl.ds(below * SUB + t, rest, stride=SUB), :]
                work[pl.ds(below * SUB + t, rest, stride=SUB), :] = (
                    jnp.where(done, 0.0, old) - update
                )


def products(first, u_parts, tv, pu, v_parts):
    new_u = jnp.dot(
        jnp.concatenate([first, first], axis=1), u_parts, preferred_element_type=F32
    ).astype(BF16)
    right = jnp.concatenate([tv, pu], axis=1)
    new_v = (
        jnp.dot(right, v_parts[0], preferred_element_type=F32)
        + jnp.dot(right, v_parts[1], preferred_element_type=F32)
    ).astype(BF16)
    return new_u, new_v


def tile_kernel(
    tile_rank, band_rank, row_rank, target_rank,
    tile_u, tile_v, all_ru, all_rv, all_pu, all_pv, new_u, new_v,
    work, left, gram_t, gram_r,
):
    tiles, order, width = tile_u.shape[1:]
    ru = all_ru[...]
    rv = all_rv[...]
    rr = row_rank[0]
    row = lax.broadcasted_iota(jnp.int32, (width, width), 0)
    for t in range(tiles):
        first_half(t, tile_u[0, t], ru, tile_rank[0, t], rr, left, gram_t, gram_r, work)
    eliminate(work, width, tiles)
    for t in range(tiles):
        core = jnp.where(row < rr, across(rv, all_pv[:, t].reshape(order, width)), 0.0)
        ranks = (tile_rank[0, t], band_rank[t], target_rank[0, t])
        u_parts, v_parts = factors(t, math.sqrt(order), ranks, core, gram_t, gram_r, work)
        new_u[0, t], new_v[0, t] = products(
            left[t], jnp.concatenate(u_parts, axis=0), tile_v[0, t],
            all_pu[:, t].reshape(order, width), v_parts,
        )


def factor_kernel(
    n_blk, n_col, tile_rank, band_rank, row_rank, target_rank, tile_u, ru, rv, pu, pv,
    all_pu, left_out, u_out, v_out,
    tu, own_ru, near_ru, far_ru, all_ru, all_rv, all_pv, left, work, gram_t, gram_r, cores,
    own_sem, tile_sem, left_sem, col_send, col_recv, blk_send, blk_recv, pair_send, pair_recv,
):
    tiles, order, width = tu.shape
    b, c = lax.axis_index("blk"), lax.axis_index("col")
    group, side = b // 2, b % 2
    sibling = group * 2 + 1 - side
    near = {step: flip(group, step) * 2 + side for step in (1, 2, 3)}

    barrier = pltpu.get_barrier_semaphore()
    peers = [(b, (c + step) % n_col) for step in range(1, n_col)]
    peers += [(near[1], c), (near[2], c), (sibling, c)]
    for peer in peers:
        pl.semaphore_signal(barrier, inc=1, device_id=peer, device_id_type=MESH)

    locals_ = [
        pltpu.make_async_copy(ru.at[0], own_ru, own_sem.at[0]),
        pltpu.make_async_copy(rv.at[0], all_rv.at[c], own_sem.at[1]),
        pltpu.make_async_copy(pv, all_pv.at[b], own_sem.at[2]),
        pltpu.make_async_copy(pu, all_pu.at[b], own_sem.at[3]),
    ]
    tile_copies = [
        pltpu.make_async_copy(tile_u.at[0, t], tu.at[t], tile_sem.at[t]) for t in range(tiles)
    ]
    for copy in locals_ + tile_copies:
        copy.start()

    pl.semaphore_wait(barrier, len(peers))

    def row_sends(at, source, whole):
        copies = [
            pltpu.make_async_remote_copy(
                src_ref=source,
                dst_ref=whole.at[c],
                send_sem=col_send.at[at, step],
                recv_sem=col_recv.at[at, step],
                device_id=(b, (c + step) % n_col),
                device_id_type=MESH,
            )
            for step in range(1, n_col)
        ]
        for copy in copies:
            copy.start()
        return copies

    def panel_send(at, step, source, whole, slot, target, send, recv):
        copy = pltpu.make_async_remote_copy(
            src_ref=source,
            dst_ref=whole.at[slot],
            send_sem=send.at[at, step],
            recv_sem=recv.at[at, step],
            device_id=(target, c),
            device_id_type=MESH,
        )
        copy.start()
        return copy

    wholes = (all_pv, all_pu)
    blk_copies, pair_copies = {}, []
    for at, source in enumerate((pv, pu)):
        for step in (1, 2):
            blk_copies[at, step] = panel_send(
                at, step, source, wholes[at], b, near[step], blk_send, blk_recv
            )
    for at, source in enumerate((pv, pu)):
        pair_copies.append(
            panel_send(at, 0, source, wholes[at], b, sibling, pair_send, pair_recv)
        )

    chunk = order // n_col
    part, half = chunk // 2, width // 2
    row = lax.broadcasted_iota(jnp.int32, (width, width), 0)
    col = lax.broadcasted_iota(jnp.int32, (width, width), 1)
    place = col // 2
    even = col % 2 == 0

    def one_hot(*blocks):
        return jnp.concatenate([block.astype(BF16) for block in blocks], axis=0)

    locals_[0].wait()
    mine = jnp.concatenate([own_ru[:part, :], own_ru[part:, :]], axis=1)
    low = col < half
    for whole, shift in ((near_ru, 0), (far_ru, half)):
        whole[c] = jnp.dot(
            mine,
            one_hot((row == col + shift) & low, (row == col - half + shift) & jnp.logical_not(low)),
            preferred_element_type=F32,
        ).astype(BF16)

    near_copies = row_sends(0, near_ru.at[c], near_ru)

    def pass_on(at, step):
        blk_copies[at, step].wait_recv()
        slot = near[step]
        here = wholes[at].at[slot]
        if (at, step) == (0, 2):
            blk_copies[0, 3] = panel_send(0, 3, here, all_pv, slot, near[1], blk_send, blk_recv)
        if (at, step) == (1, 1):
            blk_copies[1, 3] = panel_send(1, 3, here, all_pu, slot, near[2], blk_send, blk_recv)
        pair_copies.append(
            panel_send(at, step, here, wholes[at], slot, sibling, pair_send, pair_recv)
        )

    for copy in near_copies:
        copy.wait_recv()
    far_copies = row_sends(1, far_ru.at[c], far_ru)
    rv_copies = row_sends(2, rv.at[0], all_rv)
    rr = row_rank[0]
    left_copies = []
    for t in range(tiles):
        tr = tile_rank[0, t]
        tile_copies[t].wait()
        pick_t = (row == place) & even & (row < tr)
        for side_by in range(2):
            pick_r = (row - side_by * half == place) & jnp.logical_not(even) & (place < rr)
            starts = [q * chunk + side_by * part for q in range(n_col)]
            both = jnp.concatenate(
                [
                    jnp.concatenate([tu[t, start : start + part, :], near_ru[q]], axis=1)
                    for q, start in enumerate(starts)
                ],
                axis=0,
            )
            first = jnp.dot(both, one_hot(pick_t, pick_r), preferred_element_type=F32)
            first = first.astype(BF16)
            for q, start in enumerate(starts):
                left[t, start : start + part, :] = first[q * part : (q + 1) * part]
        first = left[t]
        spare = (row == col) & (place >= jnp.where(even, tr, rr))
        work[pl.ds(t, width, stride=SUB), :] = across(first, first) + spare.astype(F32)
    for t in range(tiles):
        copy = pltpu.make_async_copy(left.at[t], left_out.at[t], left_sem.at[t])
        copy.start()
        left_copies.append(copy)

    def neighbours():
        for at, step in ((0, 2), (1, 1), (0, 1), (1, 2)):
            pass_on(at, step)
        for t in range(tiles):
            gram_t[t] = across(tu[t], left[t])

    def row_grams():
        for copy in far_copies:
            copy.wait_recv()
        for side_by in range(2):
            back = one_hot(
                (row - side_by * half == col) & low,
                (row - side_by * half == col - half) & jnp.logical_not(low),
            )
            for q in range(n_col):
                both = jnp.concatenate([near_ru[q], far_ru[q]], axis=1)
                start = q * chunk + side_by * part
                all_ru[start : start + part, :] = jnp.dot(
                    both, back, preferred_element_type=F32
                ).astype(BF16)
        for t in range(tiles):
            gram_r[t] = across(all_ru[...], left[t])

    def diagonal():
        pass_on(0, 3)
        pass_on(1, 3)

    eliminate(
        work, width, tiles, {SUPER: neighbours, 2 * SUPER: row_grams, 3 * SUPER: diagonal}
    )
    for copy in locals_[1:]:
        copy.wait()
    for copy in rv_copies + pair_copies:
        copy.wait_recv()
    rv_all = all_rv[...].reshape(order, width)
    for t in range(tiles):
        cores[t] = jnp.where(
            row < rr, across(rv_all, all_pv[:, t].reshape(order, width)), 0.0
        )
    for t in range(tiles):
        ranks = (tile_rank[0, t], band_rank[t], target_rank[0, t])
        u_parts, v_parts = factors(t, math.sqrt(order), ranks, cores[t], gram_t, gram_r, work)
        u_out[t] = jnp.concatenate(u_parts, axis=0)
        v_out[t, 0], v_out[t, 1] = v_parts
    for copy in left_copies:
        copy.wait()
    for copy in near_copies + far_copies + rv_copies + list(blk_copies.values()) + pair_copies:
        copy.wait_send()


def factor(n_blk, n_col, tile_u, tile_rank, panel_u, panel_v, band_rank, row_u, row_v, row_rank, target_rank):
    tiles, order, width = tile_u.shape[1:]
    smem = pl.BlockSpec(memory_space=pltpu.SMEM)
    vmem = pl.BlockSpec(memory_space=pltpu.VMEM)
    any_space = pl.BlockSpec(memory_space=pl.ANY)
    dma = pltpu.SemaphoreType.DMA
    row_shape = (n_col,) + row_u.shape[1:]
    panel_shape = (n_blk,) + panel_u.shape
    packed = (n_col, row_u.shape[1] // 2, width)
    return pl.pallas_call(
        functools.partial(factor_kernel, n_blk, n_col),
        out_shape=[
            jax.ShapeDtypeStruct(panel_shape, BF16),
            jax.ShapeDtypeStruct((tiles, order, width), BF16),
            jax.ShapeDtypeStruct((tiles, 2 * width, width), BF16),
            jax.ShapeDtypeStruct((tiles, 2, 2 * width, width), BF16),
        ],
        in_specs=[smem] * 4 + [pl.BlockSpec(memory_space=pltpu.HBM)] * 5,
        out_specs=[any_space] * 2 + [vmem] * 2,
        scratch_shapes=[
            pltpu.VMEM((tiles, order, width), BF16),
            pltpu.VMEM(row_u.shape[1:], BF16),
            pltpu.VMEM(packed, BF16),
            pltpu.VMEM(packed, BF16),
            pltpu.VMEM((order, width), BF16),
            pltpu.VMEM(row_shape, BF16),
            pltpu.VMEM(panel_shape, BF16),
            pltpu.VMEM((tiles, order, width), BF16),
            pltpu.VMEM((width * SUB, width), F32),
            pltpu.VMEM((tiles, width, width), F32),
            pltpu.VMEM((tiles, width, width), F32),
            pltpu.VMEM((tiles, width, width), F32),
            dma((4,)),
            dma((tiles,)),
            dma((tiles,)),
            dma((3, n_col)),
            dma((3, n_col)),
            dma((2, 4)),
            dma((2, 4)),
            dma((2, 4)),
            dma((2, 4)),
        ],
        compiler_params=pltpu.CompilerParams(
            collective_id=0, has_side_effects=True, vmem_limit_bytes=60 * 1024 * 1024
        ),
        name="factor",
    )(tile_rank, band_rank, row_rank, target_rank, tile_u, row_u, row_v, panel_u, panel_v)


def product_kernel(left, u_parts, tile_v, all_pu, v_parts, new_u, new_v):
    order, width = left.shape[1:]
    new_u[0, 0], new_v[0, 0] = products(
        left[0], u_parts[0], tile_v[0, 0], all_pu[:, 0].reshape(order, width), v_parts[0]
    )


def product(left, u_parts, tile_v, all_pu, v_parts):
    tiles, order, width = left.shape
    tile = pl.BlockSpec((1, 1, order // 2, width), lambda t, h: (0, t, h, 0))
    n_blk, _, rows, _ = all_pu.shape
    return pl.pallas_call(
        product_kernel,
        grid=(tiles, 2),
        out_shape=[jax.ShapeDtypeStruct(tile_v.shape, BF16)] * 2,
        in_specs=[
            pl.BlockSpec((1, order // 2, width), lambda t, h: (t, h, 0)),
            pl.BlockSpec((1, 2 * width, width), lambda t, h: (t, 0, 0)),
            tile,
            pl.BlockSpec((n_blk // 2, 1, rows, width), lambda t, h: (h, t, 0, 0)),
            pl.BlockSpec((1, 2, 2 * width, width), lambda t, h: (t, 0, 0, 0)),
        ],
        out_specs=[tile] * 2,
        compiler_params=pltpu.CompilerParams(vmem_limit_bytes=60 * 1024 * 1024),
        name="product",
    )(left, u_parts, tile_v, all_pu, v_parts)


def update(tile_u, tile_v, tile_rank, all_pu, all_pv, band_rank, all_ru, all_rv, row_rank, target_rank):
    tiles, order, width = tile_u.shape[1:]
    smem = pl.BlockSpec(memory_space=pltpu.SMEM)
    vmem = pl.BlockSpec(memory_space=pltpu.VMEM)
    return pl.pallas_call(
        tile_kernel,
        out_shape=[jax.ShapeDtypeStruct(tile_u.shape, BF16)] * 2,
        in_specs=[smem] * 4 + [vmem] * 6,
        out_specs=[vmem] * 2,
        scratch_shapes=[
            pltpu.VMEM((width * SUB, width), F32),
            pltpu.VMEM((tiles, order, width), BF16),
            pltpu.VMEM((tiles, width, width), F32),
            pltpu.VMEM((tiles, width, width), F32),
        ],
        compiler_params=pltpu.CompilerParams(vmem_limit_bytes=48 * 1024 * 1024),
        name="tiles",
    )(tile_rank, band_rank, row_rank, target_rank, tile_u, tile_v, all_ru, all_rv, all_pu, all_pv)


def on_device(
    n_blk, n_col,
    tile_u, tile_v, tile_rank, panel_u, panel_v, band_rank, row_u, row_v, row_rank, target_rank,
):
    order, width = tile_u.shape[2:]
    if n_blk == 8 and panel_u.shape[1] % 16 == 0:
        all_pu, left, u_parts, v_parts = factor(
            n_blk, n_col, tile_u, tile_rank, panel_u, panel_v, band_rank, row_u, row_v, row_rank,
            target_rank,
        )
        return tuple(product(left, u_parts, tile_v, all_pu, v_parts))
    all_ru, all_rv, all_pu, all_pv = gather(n_blk, n_col, row_u, row_v, panel_u, panel_v)
    all_ru, all_rv = all_ru.reshape(order, width), all_rv.reshape(order, width)
    if panel_u.shape[1] % 16:
        all_pu, all_pv = (
            jnp.swapaxes(each, 0, 1).reshape(1, each.shape[1], order, width)
            for each in (all_pu, all_pv)
        )
    return tuple(
        update(
            tile_u, tile_v, tile_rank, all_pu, all_pv, band_rank, all_ru, all_rv, row_rank,
            target_rank,
        )
    )


def solution(mesh):
    return jax.shard_map(
        functools.partial(on_device, mesh.shape["blk"], mesh.shape["col"]),
        mesh=mesh,
        in_specs=(
            P("blk", "col", None, None),
            P("blk", "col", None, None),
            P("blk", "col"),
            P("col", "blk", None),
            P("col", "blk", None),
            P("col"),
            P("blk", "col", None),
            P("blk", "col", None),
            P("blk"),
            P("blk", "col"),
        ),
        out_specs=(P("blk", "col", None, None), P("blk", "col", None, None)),
        check_vma=False,
    )
```
